32 devices in a mesh: gx: 8 (over y, x, core), gy: 4 (over z).
Axes of the slice: x: 2, y: 2, z: 4, core: 2. Of those that a mesh axis runs over, the one named last changes fastest.
Arguments:
- base_state: float32 [8, 32, 2048], P(None, 'gx', 'gy'), may hold values from -6 to 6
- misfit_weight: float32 [8, 32, 2048], P(None, 'gx', 'gy'), may hold values from 0.5 to 2
- state_deltas: bfloat16 [8, 8, 32, 2048], P(None, None, 'gx', 'gy'), may hold values from -3 to 3
- delta_index: int32 [2, 8], replicated, may hold values from 0 to 7
- diag_block: float32 [2, 8, 8, 32, 2048], P(None, None, None, 'gx', 'gy'), may hold values from -2 to 24, as said below
- precond: float32 [8, 8, 32, 2048], P(None, None, 'gx', 'gy'), may hold values from -0.03 to 0.25, as said below
- face_coupling: float32 [2, 4, 8, 32, 2048], P(None, None, None, 'gx', 'gy'), may hold values from 0.2 to 1
- accumulation: float32 [8, 32, 2048], P(None, 'gx', 'gy'), may hold values from 0.5 to 2
- well_diag: float32 [512], P('gx'), may hold values from 1 to 4
- perf_well: int32 [8, 4, 128], P('gx', 'gy'), may hold values from 0 to 63
- perf_cell: int32 [8, 4, 128], P('gx', 'gy'), may hold values from 0 to 2047
- perf_coef: float32 [2, 2, 8, 8, 4, 128], P(None, None, None, 'gx', 'gy'), may hold values from -0.9 to 0.9
Outputs:
- adjoint: float32 [2, 8, 32, 2048], P(None, None, 'gx', 'gy')
The draws below stay inside these ranges and needn't reach their ends.
Inputs may be any that keep to these rules, and one draw needn't show every extreme that they name: `diag_block`: each cell's block has a dominant diagonal: diagonal entries at least 8 times the largest off-diagonal magnitude. `precond`: diagonal entries between 0.15 and 0.25, the others within -0.03 to 0.03.
All inputs are finite; a program needn't handle non-finite values.
Results may differ from the reference program's by a relative error of at most 0.0003.
Values sent between devices are 32-bit elements; how exact they have to be, the bound alone decides.
A program may use at most 64 MiB of HBM per device.

```python
import math
import jax
import jax.numpy as jnp
import numpy as np
from jax import lax

NC = 8
CX = 4
CY = 512
STEPS = 2
SWEEPS = 4
NDELTA = 8
NWELL = 64
NPERF = 128
NX = 32
NY = 2048
NWELL_ALL = 512
N_GX = 8
N_GY = 4


def draw_diag_block(key, part):
    key = jax.random.fold_in(key, 11)
    key_off, key_mid = jax.random.split(key)
    off_diag = jax.random.uniform(key_off, (STEPS, NC, NC, NX, NY), jnp.float32, -0.5, 0.5)
    diag_vals = jax.random.uniform(key_mid, (STEPS, NC, NX, NY), jnp.float32, 4.0, 6.0)
    ident = jnp.eye(NC, dtype=jnp.float32)[None, :, :, None, None]
    place = jnp.arange(NX, dtype=jnp.float32) / jnp.float32(NX - 1)
    ramp = jnp.exp(jnp.float32(1.3862944) * place)
    block = off_diag * (1.0 - ident) + ident * diag_vals[:, :, None]
    return block * ramp[None, None, None, :, None]


def draw_precond(key, part):
    key = jax.random.fold_in(key, 23)
    key_off, key_mid = jax.random.split(key)
    off_diag = jax.random.uniform(key_off, (NC, NC, NX, NY), jnp.float32, -0.03, 0.03)
    diag_vals = jax.random.uniform(key_mid, (NC, NX, NY), jnp.float32, 0.15, 0.25)
    ident = jnp.eye(NC, dtype=jnp.float32)[:, :, None, None]
    return off_diag * (1.0 - ident) + ident * diag_vals[:, None]


def place_ends(result, own_key, least, top_value):
    dims = result.shape
    spot = [jax.random.randint(jax.random.fold_in(own_key, axis), (), 0, dims[axis]) for axis in range(len(dims))]
    result = result.at[tuple(spot)].set(least)
    longest = dims.index(max(dims))
    spot[longest] = (spot[longest] + 1) % dims[longest]
    return result.at[tuple(spot)].set(top_value)


def steps_of(stream_key, shape, shards, least, largest):
    loudness = 1.0
    for position, parts in shards:
        steps = jax.random.uniform(jax.random.fold_in(jax.random.fold_in(stream_key, 6), position), (parts,), jnp.float32, least / len(shards), largest / len(shards))
        loudness = loudness * jnp.repeat(jnp.exp(steps), shape[position] // parts).reshape((-1,) + (1,) * (len(shape) - 1 - position))
    return loudness


def rank_bounds(number_of, skew):
    loads = [(1 << 20) // math.isqrt(standing ** skew) + 1 for standing in range(1, number_of + 1)]
    spread = 1 + sum(loads) // (1 << 30)
    return np.cumsum(np.array([max(1, weight // spread) for weight in loads]))


def ranked(stream_key, shape, count, skew):
    grid = rank_bounds(count, skew)
    pick = jax.random.randint(jax.random.fold_in(stream_key, 1), shape, 0, int(grid[count - 1]))
    grade = jnp.searchsorted(jnp.asarray(grid, jnp.int32), pick, side="right")
    return jax.random.permutation(jax.random.fold_in(stream_key, 2), count)[grade].astype(jnp.int32)


def noise(stream_key, extent, scale, bound, cuts=(), held_as=jnp.bfloat16):
    factor_of = steps_of(stream_key, extent, cuts, -0.22, 0.18) if cuts else 1.0
    entries = jax.random.normal(stream_key, extent, jnp.float32) * scale * factor_of
    return jnp.minimum(jnp.maximum(entries, -bound), bound).astype(held_as)


def setup_inputs(seed: int = 0) -> dict:
    streams_of = jax.random.split(jax.random.key(seed), 13)
    base_state = noise(streams_of[0], (NC, NX, NY), 1.0, 6.0, ((1, 8), (2, 4)), jnp.float32)
    misfit_weight = jnp.clip(jnp.exp(math.log(2.0) - 1.3862944 * jax.random.uniform(streams_of[1], (NC, NX, NY), jnp.float32) ** steps_of(streams_of[1], (NC, NX, NY), ((1, 8), (2, 4)), -0.2, 0.2)), 0.5, 2.0)
    state_deltas = noise(streams_of[2], (NDELTA, NC, NX, NY), 0.5, 3.0, ((2, 8), (3, 4)))
    delta_index = place_ends(jax.random.randint(streams_of[3], (STEPS, NC), 0, NDELTA), jax.random.fold_in(streams_of[3], 1), 0, NDELTA - 1).astype(jnp.int32)
    diag_block = draw_diag_block(jax.random.fold_in(streams_of[12], 71), 0)
    precond = draw_precond(jax.random.fold_in(streams_of[12], 71), 0)
    face_coupling = jnp.clip(0.2 + 0.8 * jax.random.uniform(streams_of[6], (STEPS, 4, NC, NX, NY), jnp.float32) ** steps_of(streams_of[6], (STEPS, 4, NC, NX, NY), ((3, 8), (4, 4)), -0.2, 0.2), 0.2, 1.0)
    accumulation = jnp.clip(jnp.exp(math.log(2.0) - 1.3862944 * jax.random.uniform(streams_of[7], (NC, NX, NY), jnp.float32) ** steps_of(streams_of[7], (NC, NX, NY), ((1, 8), (2, 4)), -0.2, 0.2)), 0.5, 2.0)
    well_diag = jnp.clip(jnp.exp(math.log(4.0) - 1.3862944 * jax.random.uniform(streams_of[8], (NWELL_ALL,), jnp.float32) ** steps_of(streams_of[8], (NWELL_ALL,), ((0, 8),), -0.2, 0.2)), 1.0, 4.0)
    perf_well = place_ends(ranked(streams_of[9], (N_GX, N_GY, NPERF), NWELL, 2), jax.random.fold_in(streams_of[9], 3), 0, NWELL - 1).astype(jnp.int32)
    perf_cell = place_ends(jax.random.randint(streams_of[10], (N_GX, N_GY, NPERF), 0, CX * CY), jax.random.fold_in(streams_of[10], 1), 0, (CX * CY) - 1).astype(jnp.int32)
    perf_coef = noise(streams_of[11], (STEPS, 2, NC, N_GX, N_GY, NPERF), 0.15, 0.9, ((3, 8), (4, 4)), jnp.float32)
    return {"base_state": base_state, "misfit_weight": misfit_weight, "state_deltas": state_deltas, "delta_index": delta_index, "diag_block": diag_block, "precond": precond, "face_coupling": face_coupling, "accumulation": accumulation, "well_diag": well_diag, "perf_well": perf_well, "perf_cell": perf_cell, "perf_coef": perf_coef}


def neighbour_term(field, coupling):
    padded_v = jnp.pad(field, ((0, 0), (1, 1), (1, 1)))
    padded_c = jnp.pad(coupling, ((0, 0), (0, 0), (1, 1), (1, 1)))
    total = padded_c[1, :, :-2, 1:-1] * padded_v[:, :-2, 1:-1]
    total = total + padded_c[0, :, 2:, 1:-1] * padded_v[:, 2:, 1:-1]
    total = total + padded_c[3, :, 1:-1, :-2] * padded_v[:, 1:-1, :-2]
    total = total + padded_c[2, :, 1:-1, 2:] * padded_v[:, 1:-1, 2:]
    return total


def select_delta(state_deltas, chosen):
    count = state_deltas.shape[0]
    match = chosen[None, :] == jnp.arange(count, dtype=jnp.int32)[:, None]
    return jnp.sum(jnp.where(match[:, :, None, None], state_deltas.astype(jnp.float32), jnp.float32(0.0)), axis=0)


def reference(base_state, misfit_weight, state_deltas, delta_index, diag_block, precond, face_coupling, accumulation, well_diag, perf_well, perf_cell, perf_coef):
    high = lax.Precision.HIGHEST
    comps = base_state.shape[0]
    index_x = jnp.arange(N_GX, dtype=jnp.int32)[:, None, None]
    index_y = jnp.arange(N_GY, dtype=jnp.int32)[None, :, None]
    cell_x = (index_x * CX + perf_cell // CY).reshape(-1)
    cell_y = (index_y * CY + perf_cell % CY).reshape(-1)
    well_ids = (index_x * NWELL + perf_well).reshape(-1)
    states = []
    running = base_state
    for step_no in range(STEPS):
        running = running + select_delta(state_deltas, delta_index[step_no])
        states.append(running)

    def apply_op(field, step_no):
        row_coef = perf_coef[step_no, 0].reshape(comps, -1)
        col_coef = perf_coef[step_no, 1].reshape(comps, -1)
        picked = field[:, cell_x, cell_y]
        weighted = jnp.sum(row_coef * picked, axis=0)
        well_adj = jax.ops.segment_sum(weighted, well_ids, num_segments=NWELL * N_GX) / well_diag
        wells = jnp.zeros_like(field).at[:, cell_x, cell_y].add(col_coef * well_adj[well_ids][None, :])
        diag_part = jnp.einsum("jixy,jxy->ixy", diag_block[step_no], field, precision=high)
        return diag_part - neighbour_term(field, face_coupling[step_no]) - wells

    results = [None] * STEPS
    for step_no in range(STEPS - 1, -1, -1):
        rhs = misfit_weight * states[step_no]
        if step_no < STEPS - 1:
            rhs = rhs + accumulation * results[step_no + 1]
        solution = jnp.zeros_like(rhs)
        residual = rhs
        for sweep in range(SWEEPS):
            search = jnp.einsum("ijxy,jxy->ixy", precond, residual, precision=high)
            image = apply_op(search, step_no)
            step_len = jnp.sum(residual * image) / jnp.sum(image * image)
            solution = solution + step_len * search
            residual = residual - step_len * image
        results[step_no] = solution
    return jnp.stack(results)
```

```python
import functools

import jax
import jax.numpy as jnp
from jax import lax
from jax.experimental import pallas as pl
from jax.experimental.pallas import tpu as pltpu
from jax.sharding import PartitionSpec as P

SWEEPS = 4
LANES = 128
MESH = pl.DeviceIdType.MESH


def split3(x):
    a = x.astype(jnp.bfloat16)
    rest = x - a.astype(jnp.float32)
    b = rest.astype(jnp.bfloat16)
    c = (rest - b.astype(jnp.float32)).astype(jnp.bfloat16)
    return jnp.concatenate([a, b, c], axis=0)


def exact_dot(x, sel, transposed=False):
    rows = x.shape[0]
    dims = (((1,), (1 if transposed else 0,)), ((), ()))
    out = lax.dot_general(split3(x), sel, dims, preferred_element_type=jnp.float32)
    return out[:rows] + out[rows : 2 * rows] + out[2 * rows :]


def kernel(
    ngx,
    ngy,
    comps,
    nx,
    nch,
    nwells,
    steps,
    base_hbm,
    weight_hbm,
    deltas_hbm,
    index_ref,
    diag_hbm,
    precond_hbm,
    face_hbm,
    accum_hbm,
    wdiag_ref,
    pwell_ref,
    pcell_ref,
    pcoef_ref,
    out_ref,
    base,
    weight,
    deltas,
    diag,
    precond,
    face,
    accum,
    acc,
    edge,
    xlo_out,
    xhi_out,
    ylo_out,
    yhi_out,
    xlo_in,
    xhi_in,
    ylo_in,
    yhi_in,
    gy_buf,
    gx_buf,
    load_sem,
    send_sem,
    xlo_sem,
    xhi_sem,
    ylo_sem,
    yhi_sem,
    gy_sem,
    gx_sem,
):
    rows = nx * nch
    cells = (comps, rows, LANES)
    flat = (comps * rows, LANES)
    rounds = steps * (SWEEPS + 1)
    mx = lax.axis_index("gx")
    my = lax.axis_index("gy")
    has_xlo, has_xhi = mx > 0, mx < ngx - 1
    has_ylo, has_yhi = my > 0, my < ngy - 1

    loads = []
    order = (
        (base_hbm, base),
        (weight_hbm, weight),
        (deltas_hbm, deltas),
        (precond_hbm, precond),
        (face_hbm, face),
        (diag_hbm, diag),
        (accum_hbm, accum),
    )
    for n, (src, dst) in enumerate(order):
        cp = pltpu.make_async_copy(src, dst, load_sem.at[n])
        cp.start()
        loads.append(cp)

    barrier = pltpu.get_barrier_semaphore()
    for d in range(1, ngx):
        pl.semaphore_signal(
            barrier, inc=1, device_id=(lax.rem(mx + d, ngx), my), device_id_type=MESH
        )
    for d in range(1, ngy):
        pl.semaphore_signal(
            barrier, inc=1, device_id=(mx, lax.rem(my + d, ngy)), device_id_type=MESH
        )

    @pl.when(jnp.logical_not(has_xlo))
    def _():
        xlo_in[...] = jnp.zeros_like(xlo_in)

    @pl.when(jnp.logical_not(has_xhi))
    def _():
        xhi_in[...] = jnp.zeros_like(xhi_in)

    @pl.when(jnp.logical_not(has_ylo))
    def _():
        ylo_in[...] = jnp.zeros_like(ylo_in)

    @pl.when(jnp.logical_not(has_yhi))
    def _():
        yhi_in[...] = jnp.zeros_like(yhi_in)

    pcell = pcell_ref[0]
    length_y = nch * LANES
    p_lane = lax.rem(pcell, LANES)
    p_row = lax.rem(lax.div(pcell, LANES), nch) * nx + lax.div(pcell, length_y)
    nperf = pcell.shape[-1]
    lane_sel = (
        (lax.broadcasted_iota(jnp.int32, (LANES, nperf), 0) == p_lane)
        .astype(jnp.float32)
        .astype(jnp.bfloat16)
    )
    row_mask = lax.broadcasted_iota(jnp.int32, (rows, nperf), 0) == p_row
    well_mask = lax.broadcasted_iota(jnp.int32, (LANES, nperf), 0) == pwell_ref[0]
    well_sel = well_mask.astype(jnp.float32).astype(jnp.bfloat16)
    lane_ids = lax.broadcasted_iota(jnp.int32, (1, rows, LANES), 2)
    row_ids = lax.broadcasted_iota(jnp.int32, (1, rows, LANES), 1)
    sub_ids = lax.broadcasted_iota(jnp.int32, (8, LANES), 0)
    x_ids = lax.rem(row_ids, nx)

    loads[0].wait()
    loads[1].wait()
    loads[2].wait()
    states = []
    running = base[...]
    for k in range(steps):
        picked = [
            deltas[index_ref[k, c], c].astype(jnp.float32)[None] for c in range(comps)
        ]
        running = running + jnp.concatenate(picked, axis=0)
        states.append(running)

    def spread(c_row):
        full = jnp.where(row_mask[None], c_row[:, None, :], jnp.float32(0.0))
        return full.reshape(comps * rows, nperf)

    def apply_precond(v):
        total = precond[:, 0] * v[0][None]
        for j in range(1, comps):
            total = total + precond[:, j] * v[j][None]
        return total

    def neighbour_copy(src, dst, sem_out, sem_in, target):
        return pltpu.make_async_remote_copy(
            src_ref=src,
            dst_ref=dst,
            send_sem=sem_out,
            recv_sem=sem_in,
            device_id=target,
            device_id_type=MESH,
        )

    def wait_bytes(ref, sem):
        pltpu.make_async_copy(ref, ref, sem).wait()

    def operator(k, rnd, v, row_w, col_w, dots):
        f_hi = face[k, 1] * v
        edge[...] = f_hi.reshape(flat)
        xhi_out[rnd] = edge[pl.ds(nx - 1, comps * nch, stride=nx), :]

        @pl.when(has_xhi)
        def _():
            neighbour_copy(
                xhi_out.at[rnd], xlo_in.at[rnd], send_sem.at[0], xlo_sem.at[rnd], (mx + 1, my)
            ).start()

        f_lo = face[k, 0] * v
        edge[...] = f_lo.reshape(flat)
        xlo_out[rnd] = edge[pl.ds(0, comps * nch, stride=nx), :]

        @pl.when(has_xlo)
        def _():
            neighbour_copy(
                xlo_out.at[rnd], xhi_in.at[rnd], send_sem.at[1], xhi_sem.at[rnd], (mx - 1, my)
            ).start()

        g = pltpu.roll((face[k, 3] * v).reshape(flat), 1, axis=1).reshape(cells)
        wrap = jnp.concatenate([g[:, rows - nx :], g[:, : rows - nx]], axis=1)
        is_lane = lane_ids == 0
        is_rim = jnp.logical_and(is_lane, row_ids < nx)
        yhi_out[rnd] = jnp.where(is_lane[:, :nx], wrap[:, :nx], 0.0).reshape(comps * nx, LANES)

        @pl.when(has_yhi)
        def _():
            neighbour_copy(
                yhi_out.at[rnd], ylo_in.at[rnd], send_sem.at[2], ylo_sem.at[rnd], (mx, my + 1)
            ).start()

        from_ylo = jnp.where(is_rim, 0.0, jnp.where(is_lane, wrap, g))
        g = pltpu.roll((face[k, 2] * v).reshape(flat), LANES - 1, axis=1).reshape(cells)
        wrap = jnp.concatenate([g[:, nx:], g[:, :nx]], axis=1)
        is_lane = lane_ids == LANES - 1
        is_rim = jnp.logical_and(is_lane, row_ids >= rows - nx)
        ylo_out[rnd] = jnp.where(is_lane[:, rows - nx :], wrap[:, rows - nx :], 0.0).reshape(
            comps * nx, LANES
        )

        @pl.when(has_ylo)
        def _():
            neighbour_copy(
                ylo_out.at[rnd], yhi_in.at[rnd], send_sem.at[3], yhi_sem.at[rnd], (mx, my - 1)
            ).start()

        from_yhi = jnp.where(is_rim, 0.0, jnp.where(is_lane, wrap, g))

        picked = exact_dot(v.reshape(flat), lane_sel)
        weighted = jnp.sum(row_w * picked, axis=0, keepdims=True)
        well_part = exact_dot(jnp.broadcast_to(weighted, (8, nperf)), well_sel, transposed=True)
        message = jnp.where(sub_ids == 0, well_part, 0.0)
        message = add_dots(message, dots)
        start_gy(rnd, message)

        total = diag[k, 0] * v[0][None]
        for j in range(1, comps):
            total = total + diag[k, j] * v[j][None]
        down = jnp.concatenate([f_hi[:, rows - 1 :], f_hi[:, : rows - 1]], axis=1)
        up = jnp.concatenate([f_lo[:, 1:], f_lo[:, :1]], axis=1)
        total = total - from_ylo - from_yhi
        total = total - jnp.where(x_ids == 0, 0.0, down)
        total = total - jnp.where(x_ids == nx - 1, 0.0, up)
        acc[...] = total.reshape(flat)

        summed = end_gy(rnd)
        if dots is not None:
            start_gx(rnd, summed)
        per_well = jnp.where(sub_ids == 0, summed * inv_well, 0.0)
        per_perf = jnp.sum(exact_dot(per_well, well_sel), axis=0, keepdims=True)
        moved = exact_dot(col_w * per_perf, lane_sel, transposed=True)

        @pl.when(has_xlo)
        def _():
            wait_bytes(xlo_in.at[rnd], xlo_sem.at[rnd])

        @pl.when(has_xhi)
        def _():
            wait_bytes(xhi_in.at[rnd], xhi_sem.at[rnd])

        @pl.when(has_ylo)
        def _():
            wait_bytes(ylo_in.at[rnd], ylo_sem.at[rnd])

        @pl.when(has_yhi)
        def _():
            wait_bytes(yhi_in.at[rnd], yhi_sem.at[rnd])

        acc[...] = acc[...] - moved
        lo_rows = pl.ds(0, comps * nch, stride=nx)
        hi_rows = pl.ds(nx - 1, comps * nch, stride=nx)
        acc[lo_rows, :] = acc[lo_rows, :] - xlo_in[rnd]
        acc[hi_rows, :] = acc[hi_rows, :] - xhi_in[rnd]
        for c in range(comps):
            first = pl.ds(c * rows, nx)
            last = pl.ds(c * rows + rows - nx, nx)
            part = pl.ds(c * nx, nx)
            acc[first, :] = acc[first, :] - ylo_in[rnd, part, :]
            acc[last, :] = acc[last, :] - yhi_in[rnd, part, :]
        return acc[...].reshape(cells)

    def add_dots(message, dots):
        if dots is None:
            return message
        a, b = dots
        a = jnp.sum(a.reshape(flat), axis=0, keepdims=True)
        b = jnp.sum(b.reshape(flat), axis=0, keepdims=True)
        return jnp.where(sub_ids == 1, a, jnp.where(sub_ids == 2, b, message))

    def start_gy(rnd, message):
        gy_buf[rnd, my] = message
        for d in range(1, ngy):
            neighbour_copy(
                gy_buf.at[rnd, my],
                gy_buf.at[rnd, my],
                send_sem.at[4],
                gy_sem.at[rnd],
                (mx, lax.rem(my + d, ngy)),
            ).start()

    def end_gy(rnd):
        wait_bytes(gy_buf.at[rnd, pl.ds(0, ngy - 1)], gy_sem.at[rnd])
        return jnp.sum(gy_buf[rnd], axis=0)

    def start_gx(rnd, message):
        gx_buf[rnd, mx] = message
        for d in range(1, ngx):
            neighbour_copy(
                gx_buf.at[rnd, mx],
                gx_buf.at[rnd, mx],
                send_sem.at[5],
                gx_sem.at[rnd],
                (lax.rem(mx + d, ngx), my),
            ).start()

    def end_gx(rnd):
        wait_bytes(gx_buf.at[rnd, pl.ds(0, ngx - 1)], gx_sem.at[rnd])
        totals = jnp.sum(jnp.sum(gx_buf[rnd], axis=0), axis=1, keepdims=True)
        return totals[1:2] / totals[2:3]

    inv_well = jnp.float32(1.0) / wdiag_ref[...]

    loads[3].wait()
    loads[4].wait()
    loads[5].wait()
    loads[6].wait()

    pl.semaphore_wait(barrier, ngx + ngy - 2)

    adjoint = None
    rnd = 0
    for k in range(steps - 1, -1, -1):
        row_w = spread(pcoef_ref[k, 0])
        col_w = spread(pcoef_ref[k, 1])
        residual = weight[...] * states[k]
        if adjoint is not None:
            residual = residual + accum[...] * adjoint
        search = apply_precond(residual)
        image = operator(k, rnd, search, row_w, col_w, None)
        rnd += 1
        solution = None
        for sweep in range(SWEEPS):
            dots = (residual * image, image * image)
            if sweep < SWEEPS - 1:
                pre_image = apply_precond(image)
                next_image = operator(k, rnd, pre_image, row_w, col_w, dots)
            else:
                start_gy(rnd, add_dots(jnp.zeros((8, LANES), jnp.float32), dots))
                start_gx(rnd, end_gy(rnd))
            step_len = end_gx(rnd)
            rnd += 1
            moved = step_len * search.reshape(flat)
            solution = moved if solution is None else solution + moved
            if sweep < SWEEPS - 1:
                residual = residual - (step_len * image.reshape(flat)).reshape(cells)
                search = search - (step_len * pre_image.reshape(flat)).reshape(cells)
                image = image - (step_len * next_image.reshape(flat)).reshape(cells)
        adjoint = solution.reshape(cells)
        out_ref[k] = adjoint

    ops = steps * SWEEPS

    @pl.when(has_xhi)
    def _():
        wait_bytes(xhi_out.at[pl.ds(0, ops)], send_sem.at[0])

    @pl.when(has_xlo)
    def _():
        wait_bytes(xlo_out.at[pl.ds(0, ops)], send_sem.at[1])

    @pl.when(has_yhi)
    def _():
        wait_bytes(yhi_out.at[pl.ds(0, ops)], send_sem.at[2])

    @pl.when(has_ylo)
    def _():
        wait_bytes(ylo_out.at[pl.ds(0, ops)], send_sem.at[3])

    wait_bytes(gy_buf.at[:, pl.ds(0, ngy - 1)], send_sem.at[4])
    wait_bytes(gx_buf.at[pl.ds(0, ops), pl.ds(0, ngx - 1)], send_sem.at[5])


def to_rows(x):
    lead = x.shape[:-2]
    nx, ny = x.shape[-2:]
    x = x.reshape(*lead, nx, ny // LANES, LANES)
    return jnp.swapaxes(x, -3, -2).reshape(*lead, nx * (ny // LANES), LANES)


def local(
    ngx,
    ngy,
    base_state,
    misfit_weight,
    state_deltas,
    delta_index,
    diag_block,
    precond,
    face_coupling,
    accumulation,
    well_diag,
    perf_well,
    perf_cell,
    perf_coef,
):
    comps, nx, ny = base_state.shape
    nch = ny // LANES
    rows = nx * nch
    steps = diag_block.shape[0]
    nwells = well_diag.shape[0]
    nperf = perf_cell.shape[-1]
    rounds = steps * (SWEEPS + 1)
    f32 = jnp.float32
    big = [to_rows(a) for a in (base_state, misfit_weight, state_deltas)]
    big2 = [to_rows(a) for a in (diag_block, precond, face_coupling, accumulation)]
    wdiag = jnp.pad(well_diag, (0, LANES - nwells), constant_values=1.0).reshape(1, LANES)
    any_spec = pl.BlockSpec(memory_space=pl.ANY)
    vmem = pl.BlockSpec(memory_space=pltpu.VMEM)
    smem = pl.BlockSpec(memory_space=pltpu.SMEM)
    xh = pltpu.VMEM((rounds, comps * nch, LANES), f32)
    yh = pltpu.VMEM((rounds, comps * nx, LANES), f32)
    result = pl.pallas_call(
        functools.partial(kernel, ngx, ngy, comps, nx, nch, nwells, steps),
        out_shape=jax.ShapeDtypeStruct((steps, comps, rows, LANES), f32),
        in_specs=[any_spec] * 3 + [smem] + [any_spec] * 4 + [vmem] * 4,
        out_specs=vmem,
        scratch_shapes=[
            pltpu.VMEM(big[0].shape, f32),
            pltpu.VMEM(big[1].shape, f32),
            pltpu.VMEM(big[2].shape, big[2].dtype),
            pltpu.VMEM(big2[0].shape, f32),
            pltpu.VMEM(big2[1].shape, f32),
            pltpu.VMEM(big2[2].shape, f32),
            pltpu.VMEM(big2[3].shape, f32),
            pltpu.VMEM((comps * rows, LANES), f32),
            pltpu.VMEM((comps * rows, LANES), f32),
            xh,
            xh,
            yh,
            yh,
            xh,
            xh,
            yh,
            yh,
            pltpu.VMEM((rounds, ngy, 8, LANES), f32),
            pltpu.VMEM((rounds, ngx, 8, LANES), f32),
            pltpu.SemaphoreType.DMA((7,)),
            pltpu.SemaphoreType.DMA((6,)),
            pltpu.SemaphoreType.DMA((rounds,)),
            pltpu.SemaphoreType.DMA((rounds,)),
            pltpu.SemaphoreType.DMA((rounds,)),
            pltpu.SemaphoreType.DMA((rounds,)),
            pltpu.SemaphoreType.DMA((rounds,)),
            pltpu.SemaphoreType.DMA((rounds,)),
        ],
        compiler_params=pltpu.CompilerParams(
            collective_id=0, has_side_effects=True, vmem_limit_bytes=32 * 1024 * 1024
        ),
    )(
        big[0],
        big[1],
        big[2],
        delta_index,
        big2[0],
        big2[1],
        big2[2],
        big2[3],
        wdiag,
        perf_well.reshape(1, 1, nperf),
        perf_cell.reshape(1, 1, nperf),
        perf_coef.reshape(steps, 2, comps, nperf),
    )
    result = result.reshape(steps, comps, nch, nx, LANES)
    return jnp.swapaxes(result, -3, -2).reshape(steps, comps, nx, ny)


def solution(mesh):
    ngx, ngy = mesh.shape["gx"], mesh.shape["gy"]
    return jax.shard_map(
        functools.partial(local, ngx, ngy),
        mesh=mesh,
        in_specs=(
            P(None, "gx", "gy"),
            P(None, "gx", "gy"),
            P(None, None, "gx", "gy"),
            P(),
            P(None, None, None, "gx", "gy"),
            P(None, None, "gx", "gy"),
            P(None, None, None, "gx", "gy"),
            P(None, "gx", "gy"),
            P("gx"),
            P("gx", "gy", None),
            P("gx", "gy", None),
            P(None, None, None, "gx", "gy", None),
        ),
        out_specs=P(None, None, "gx", "gy"),
        check_vma=False,
    )
```

```python
import functools

import jax
import jax.numpy as jnp
from jax import lax
from jax.experimental import pallas as pl
from jax.experimental.pallas import tpu as pltpu
from jax.sharding import PartitionSpec as P

BATCH = 3
LANES = 128
MESH = pl.DeviceIdType.MESH


def split3(x):
    a = x.astype(jnp.bfloat16)
    rest = x - a.astype(jnp.float32)
    b = rest.astype(jnp.bfloat16)
    c = (rest - b.astype(jnp.float32)).astype(jnp.bfloat16)
    return jnp.concatenate([a, b, c], axis=0)


def exact_dot(x, sel, transposed=False):
    rows = x.shape[0]
    dims = (((1,), (1 if transposed else 0,)), ((), ()))
    out = lax.dot_general(split3(x), sel, dims, preferred_element_type=jnp.float32)
    return out[:rows] + out[rows : 2 * rows] + out[2 * rows :]


def kernel(
    ngx,
    ngy,
    comps,
    nx,
    nch,
    nwells,
    steps,
    base_hbm,
    weight_hbm,
    deltas_hbm,
    index_hbm,
    diag_hbm,
    precond_hbm,
    face_hbm,
    accum_hbm,
    wdiag_hbm,
    pwell_hbm,
    pcell_hbm,
    pcoef_hbm,
    out_ref,
    base,
    weight,
    deltas,
    diag,
    precond,
    face,
    accum,
    index_ref,
    wdiag_ref,
    pwell_ref,
    pcell_ref,
    pcoef_ref,
    acc,
    edge,
    xlo_out,
    xhi_out,
    ylo_out,
    yhi_out,
    xlo_in,
    xhi_in,
    ylo_in,
    yhi_in,
    gy_buf,
    gx_buf,
    load_sem,
    send_sem,
    xlo_sem,
    xhi_sem,
    ylo_sem,
    yhi_sem,
    gy_sem,
    gx_sem,
):
    rows = nx * nch
    cells = (comps, rows, LANES)
    flat = (comps * rows, LANES)
    mx = lax.axis_index("gx")
    my = lax.axis_index("gy")
    has_xlo, has_xhi = mx > 0, mx < ngx - 1
    has_ylo, has_yhi = my > 0, my < ngy - 1

    loads = []
    order = (
        (pcell_hbm, pcell_ref),
        (pwell_hbm, pwell_ref),
        (index_hbm, index_ref),
        (wdiag_hbm, wdiag_ref),
        (pcoef_hbm, pcoef_ref),
        (base_hbm, base),
        (weight_hbm, weight),
        (deltas_hbm, deltas),
        (precond_hbm, precond),
        (face_hbm, face),
        (diag_hbm, diag),
        (accum_hbm, accum),
    )
    for n, (src, dst) in enumerate(order):
        cp = pltpu.make_async_copy(src, dst, load_sem.at[n])
        cp.start()
        loads.append(cp)

    barrier = pltpu.get_barrier_semaphore()
    for d in range(1, ngx):
        pl.semaphore_signal(
            barrier, inc=1, device_id=(lax.rem(mx + d, ngx), my), device_id_type=MESH
        )
    for d in range(1, ngy):
        pl.semaphore_signal(
            barrier, inc=1, device_id=(mx, lax.rem(my + d, ngy)), device_id_type=MESH
        )

    @pl.when(jnp.logical_not(has_xlo))
    def _():
        xlo_in[...] = jnp.zeros_like(xlo_in)

    @pl.when(jnp.logical_not(has_xhi))
    def _():
        xhi_in[...] = jnp.zeros_like(xhi_in)

    @pl.when(jnp.logical_not(has_ylo))
    def _():
        ylo_in[...] = jnp.zeros_like(ylo_in)

    @pl.when(jnp.logical_not(has_yhi))
    def _():
        yhi_in[...] = jnp.zeros_like(yhi_in)

    loads[0].wait()
    loads[1].wait()
    pcell = pcell_ref[0]
    length_y = nch * LANES
    p_lane = lax.rem(pcell, LANES)
    p_row = lax.rem(lax.div(pcell, LANES), nch) * nx + lax.div(pcell, length_y)
    nperf = pcell.shape[-1]
    lane_sel = (
        (lax.broadcasted_iota(jnp.int32, (LANES, nperf), 0) == p_lane)
        .astype(jnp.float32)
        .astype(jnp.bfloat16)
    )
    row_mask = lax.broadcasted_iota(jnp.int32, (rows, nperf), 0) == p_row
    well_mask = lax.broadcasted_iota(jnp.int32, (LANES, nperf), 0) == pwell_ref[0]
    well_sel = well_mask.astype(jnp.float32).astype(jnp.bfloat16)
    lane_ids = lax.broadcasted_iota(jnp.int32, (1, rows, LANES), 2)
    row_ids = lax.broadcasted_iota(jnp.int32, (1, rows, LANES), 1)
    sub_ids = lax.broadcasted_iota(jnp.int32, (8, LANES), 0)
    x_ids = lax.rem(row_ids, nx)

    for n in (2, 3, 4, 5, 6, 7):
        loads[n].wait()
    states = []
    running = base[...]
    for k in range(steps):
        picked = [
            deltas[index_ref[k, c], c].astype(jnp.float32)[None] for c in range(comps)
        ]
        running = running + jnp.concatenate(picked, axis=0)
        states.append(running)

    def spread(c_row):
        full = jnp.where(row_mask[None], c_row[:, None, :], jnp.float32(0.0))
        return full.reshape(comps * rows, nperf)

    def apply_precond(v):
        total = precond[:, 0] * v[0][None]
        for j in range(1, comps):
            total = total + precond[:, j] * v[j][None]
        return total

    def neighbour_copy(src, dst, sem_out, sem_in, target):
        return pltpu.make_async_remote_copy(
            src_ref=src,
            dst_ref=dst,
            send_sem=sem_out,
            recv_sem=sem_in,
            device_id=target,
            device_id_type=MESH,
        )

    def wait_bytes(ref, sem):
        pltpu.make_async_copy(ref, ref, sem).wait()

    def operator(k, rnd, slots, vs, row_w, col_w, grams, gx_rnd):
        picked = exact_dot(jnp.concatenate([v.reshape(flat) for v in vs], axis=0), lane_sel)
        weighted = jnp.zeros((8, nperf), jnp.float32)
        for n in range(len(vs)):
            part = picked[n * comps * rows : (n + 1) * comps * rows]
            part = jnp.sum(row_w * part, axis=0, keepdims=True)
            weighted = jnp.where(sub_ids == n, part, weighted)
        start_gy(rnd, add_grams(exact_dot(weighted, well_sel, transposed=True), grams))
        kept = []
        for slot, v in zip(slots, vs):
            kept.append(send_halos(k, slot, v))

        for n, v in enumerate(vs):
            f_hi, f_lo, from_y = kept[n]
            total = diag[k, 0] * v[0][None]
            for j in range(1, comps):
                total = total + diag[k, j] * v[j][None]
            down = jnp.concatenate([f_hi[:, rows - 1 :], f_hi[:, : rows - 1]], axis=1)
            up = jnp.concatenate([f_lo[:, 1:], f_lo[:, :1]], axis=1)
            total = total - from_y
            total = total - jnp.where(x_ids == 0, 0.0, down)
            total = total - jnp.where(x_ids == nx - 1, 0.0, up)
            acc[n] = total.reshape(flat)

        for slot in slots:

            @pl.when(has_xlo)
            def _(slot=slot):
                wait_bytes(xlo_in.at[slot], xlo_sem.at[slot])

            @pl.when(has_xhi)
            def _(slot=slot):
                wait_bytes(xhi_in.at[slot], xhi_sem.at[slot])

            @pl.when(has_ylo)
            def _(slot=slot):
                wait_bytes(ylo_in.at[slot], ylo_sem.at[slot])

            @pl.when(has_yhi)
            def _(slot=slot):
                wait_bytes(yhi_in.at[slot], yhi_sem.at[slot])

        for n, slot in enumerate(slots):
            mine = acc.at[n]
            lo_rows = pl.ds(0, comps * nch, stride=nx)
            hi_rows = pl.ds(nx - 1, comps * nch, stride=nx)
            mine[lo_rows, :] = mine[lo_rows, :] - xlo_in[slot]
            mine[hi_rows, :] = mine[hi_rows, :] - xhi_in[slot]
            for c in range(comps):
                first = pl.ds(c * rows, nx)
                last = pl.ds(c * rows + rows - nx, nx)
                part = pl.ds(c * nx, nx)
                mine[first, :] = mine[first, :] - ylo_in[slot, part, :]
                mine[last, :] = mine[last, :] - yhi_in[slot, part, :]

        summed = end_gy(rnd)
        if grams is not None:
            start_gx(gx_rnd, summed)
        per_perf = exact_dot(summed * inv_well, well_sel)
        moved = [col_w * per_perf[n : n + 1] for n in range(len(vs))]
        moved = exact_dot(jnp.concatenate(moved, axis=0), lane_sel, transposed=True)
        size = comps * rows
        return [
            (acc[n] - moved[n * size : (n + 1) * size]).reshape(cells) for n in range(len(vs))
        ]

    def send_halos(k, slot, v):
        f_hi = face[k, 1] * v
        edge[0] = f_hi.reshape(flat)
        xhi_out[slot] = edge[0, pl.ds(nx - 1, comps * nch, stride=nx), :]

        @pl.when(has_xhi)
        def _():
            neighbour_copy(
                xhi_out.at[slot], xlo_in.at[slot], send_sem.at[0], xlo_sem.at[slot], (mx + 1, my)
            ).start()

        f_lo = face[k, 0] * v
        edge[1] = f_lo.reshape(flat)
        xlo_out[slot] = edge[1, pl.ds(0, comps * nch, stride=nx), :]

        @pl.when(has_xlo)
        def _():
            neighbour_copy(
                xlo_out.at[slot], xhi_in.at[slot], send_sem.at[1], xhi_sem.at[slot], (mx - 1, my)
            ).start()

        g = pltpu.roll((face[k, 3] * v).reshape(flat), 1, axis=1).reshape(cells)
        wrap = jnp.concatenate([g[:, rows - nx :], g[:, : rows - nx]], axis=1)
        is_lane = lane_ids == 0
        is_rim = jnp.logical_and(is_lane, row_ids < nx)
        yhi_out[slot] = jnp.where(is_lane[:, :nx], wrap[:, :nx], 0.0).reshape(comps * nx, LANES)

        @pl.when(has_yhi)
        def _():
            neighbour_copy(
                yhi_out.at[slot], ylo_in.at[slot], send_sem.at[2], ylo_sem.at[slot], (mx, my + 1)
            ).start()

        from_ylo = jnp.where(is_rim, 0.0, jnp.where(is_lane, wrap, g))
        g = pltpu.roll((face[k, 2] * v).reshape(flat), LANES - 1, axis=1).reshape(cells)
        wrap = jnp.concatenate([g[:, nx:], g[:, :nx]], axis=1)
        is_lane = lane_ids == LANES - 1
        is_rim = jnp.logical_and(is_lane, row_ids >= rows - nx)
        ylo_out[slot] = jnp.where(is_lane[:, rows - nx :], wrap[:, rows - nx :], 0.0).reshape(
            comps * nx, LANES
        )

        @pl.when(has_ylo)
        def _():
            neighbour_copy(
                ylo_out.at[slot], yhi_in.at[slot], send_sem.at[3], yhi_sem.at[slot], (mx, my - 1)
            ).start()

        return f_hi, f_lo, from_ylo + jnp.where(is_rim, 0.0, jnp.where(is_lane, wrap, g))

    def grams_of(q0, q1, q2):
        return (q0 * q1, q1 * q1, q0 * q2, q1 * q2, q2 * q2)

    def add_grams(message, grams):
        if grams is None:
            return message
        for n, g in enumerate(grams):
            total = jnp.sum(g.reshape(flat), axis=0, keepdims=True)
            message = jnp.where(sub_ids == BATCH + n, total, message)
        return message

    def start_gy(rnd, message):
        gy_buf[rnd, my] = message
        for d in range(1, ngy):
            neighbour_copy(
                gy_buf.at[rnd, my],
                gy_buf.at[rnd, my],
                send_sem.at[4],
                gy_sem.at[rnd],
                (mx, lax.rem(my + d, ngy)),
            ).start()

    def end_gy(rnd):
        wait_bytes(gy_buf.at[rnd, pl.ds(0, ngy - 1)], gy_sem.at[rnd])
        return jnp.sum(gy_buf[rnd], axis=0)

    def start_gx(rnd, message):
        gx_buf[rnd, mx] = message
        for d in range(1, ngx):
            neighbour_copy(
                gx_buf.at[rnd, mx],
                gx_buf.at[rnd, mx],
                send_sem.at[5],
                gx_sem.at[rnd],
                (lax.rem(mx + d, ngx), my),
            ).start()

    def end_gx(rnd):
        wait_bytes(gx_buf.at[rnd, pl.ds(0, ngx - 1)], gx_sem.at[rnd])
        totals = jnp.sum(jnp.sum(gx_buf[rnd], axis=0), axis=1, keepdims=True)
        g01, g11, g02, g12, g22 = (totals[BATCH + n : BATCH + n + 1] for n in range(5))
        first = g01 / g11
        second = (
            first * (first * g12 - g02) / (g11 - 2.0 * first * g12 + first * first * g22)
        )
        return (first + second)[None], (first * second)[None]

    inv_well = jnp.concatenate(
        [jnp.float32(1.0) / wdiag_ref[...], jnp.ones((1, LANES - nwells), jnp.float32)], axis=1
    )

    for n in (8, 9, 10, 11):
        loads[n].wait()

    pl.semaphore_wait(barrier, ngx + ngy - 2)

    gy_rnd = gx_rnd = slot = 0
    late = None
    for k in range(steps - 1, -1, -1):
        row_w = spread(pcoef_ref[k, 0])
        col_w = spread(pcoef_ref[k, 1])
        v0 = weight[...] * states[k]
        if late is None:
            u0 = apply_precond(v0)
            (v1,) = operator(k, gy_rnd, [slot], [u0], row_w, col_w, None, None)
            slot += 1
        else:
            grams, part, p0, p1 = late
            starts = [v0 + accum[...] * part, accum[...] * p0, accum[...] * p1]
            firsts = [apply_precond(v) for v in starts]
            slots = [slot + n for n in range(BATCH)]
            images = operator(k, gy_rnd, slots, firsts, row_w, col_w, grams, gx_rnd)
            slot += BATCH
            both, prod = end_gx(gx_rnd)
            gx_rnd += 1
            out_ref[k + 1] = part + both * p0 - prod * p1
            v0, u0, v1 = (a + both * b - prod * c for a, b, c in (starts, firsts, images))
        gy_rnd += 1
        u1 = apply_precond(v1)
        (v2,) = operator(k, gy_rnd, [slot], [u1], row_w, col_w, None, None)
        u2 = apply_precond(v2)
        grams = grams_of(v0, v1, v2)
        (v3,) = operator(k, gy_rnd + 1, [slot + 1], [u2], row_w, col_w, grams, gx_rnd)
        u3 = apply_precond(v3)
        (v4,) = operator(k, gy_rnd + 2, [slot + 2], [u3], row_w, col_w, None, None)
        gy_rnd += 3
        slot += 3
        both, prod = end_gx(gx_rnd)
        gx_rnd += 1
        q0 = v0 - both * v1 + prod * v2
        q1 = v1 - both * v2 + prod * v3
        q2 = v2 - both * v3 + prod * v4
        part = both * u0 - prod * u1
        p0 = u0 - both * u1 + prod * u2
        p1 = u1 - both * u2 + prod * u3
        late = grams_of(q0, q1, q2), part, p0, p1
    grams, part, p0, p1 = late
    start_gy(gy_rnd, add_grams(jnp.zeros((8, LANES), jnp.float32), grams))
    start_gx(gx_rnd, end_gy(gy_rnd))
    both, prod = end_gx(gx_rnd)
    out_ref[0] = part + both * p0 - prod * p1

    @pl.when(has_xhi)
    def _():
        wait_bytes(xhi_out, send_sem.at[0])

    @pl.when(has_xlo)
    def _():
        wait_bytes(xlo_out, send_sem.at[1])

    @pl.when(has_yhi)
    def _():
        wait_bytes(yhi_out, send_sem.at[2])

    @pl.when(has_ylo)
    def _():
        wait_bytes(ylo_out, send_sem.at[3])

    wait_bytes(gy_buf.at[:, pl.ds(0, ngy - 1)], send_sem.at[4])
    wait_bytes(gx_buf.at[:, pl.ds(0, ngx - 1)], send_sem.at[5])


def to_rows(x):
    lead = x.shape[:-2]
    nx, ny = x.shape[-2:]
    x = x.reshape(*lead, nx, ny // LANES, LANES)
    return jnp.swapaxes(x, -3, -2).reshape(*lead, nx * (ny // LANES), LANES)


def local(
    ngx,
    ngy,
    base_state,
    misfit_weight,
    state_deltas,
    delta_index,
    diag_block,
    precond,
    face_coupling,
    accumulation,
    well_diag,
    perf_well,
    perf_cell,
    perf_coef,
):
    comps, nx, ny = base_state.shape
    nch = ny // LANES
    rows = nx * nch
    steps = diag_block.shape[0]
    nwells = well_diag.shape[0]
    nperf = perf_cell.shape[-1]
    slots = 4 + (steps - 1) * (BATCH + 3)
    gy_rounds = 4 * steps + 1
    gx_rounds = 2 * steps
    f32 = jnp.float32
    big = [to_rows(a) for a in (base_state, misfit_weight, state_deltas)]
    big2 = [to_rows(a) for a in (diag_block, precond, face_coupling, accumulation)]
    any_spec = pl.BlockSpec(memory_space=pl.ANY)
    vmem = pl.BlockSpec(memory_space=pltpu.VMEM)
    xh = pltpu.VMEM((slots, comps * nch, LANES), f32)
    yh = pltpu.VMEM((slots, comps * nx, LANES), f32)
    result = pl.pallas_call(
        functools.partial(kernel, ngx, ngy, comps, nx, nch, nwells, steps),
        out_shape=jax.ShapeDtypeStruct((steps, comps, rows, LANES), f32),
        in_specs=[any_spec] * 12,
        out_specs=vmem,
        scratch_shapes=[
            pltpu.VMEM(big[0].shape, f32),
            pltpu.VMEM(big[1].shape, f32),
            pltpu.VMEM(big[2].shape, big[2].dtype),
            pltpu.VMEM(big2[0].shape, f32),
            pltpu.VMEM(big2[1].shape, f32),
            pltpu.VMEM(big2[2].shape, f32),
            pltpu.VMEM(big2[3].shape, f32),
            pltpu.SMEM(delta_index.shape, jnp.int32),
            pltpu.VMEM((1, nwells), f32),
            pltpu.VMEM((1, 1, nperf), jnp.int32),
            pltpu.VMEM((1, 1, nperf), jnp.int32),
            pltpu.VMEM((steps, 2, comps, nperf), f32),
            pltpu.VMEM((BATCH, comps * rows, LANES), f32),
            pltpu.VMEM((2, comps * rows, LANES), f32),
            xh,
            xh,
            yh,
            yh,
            xh,
            xh,
            yh,
            yh,
            pltpu.VMEM((gy_rounds, ngy, 8, LANES), f32),
            pltpu.VMEM((gx_rounds, ngx, 8, LANES), f32),
            pltpu.SemaphoreType.DMA((12,)),
            pltpu.SemaphoreType.DMA((6,)),
            pltpu.SemaphoreType.DMA((slots,)),
            pltpu.SemaphoreType.DMA((slots,)),
            pltpu.SemaphoreType.DMA((slots,)),
            pltpu.SemaphoreType.DMA((slots,)),
            pltpu.SemaphoreType.DMA((gy_rounds,)),
            pltpu.SemaphoreType.DMA((gx_rounds,)),
        ],
        compiler_params=pltpu.CompilerParams(
            collective_id=0, has_side_effects=True, vmem_limit_bytes=60 * 1024 * 1024
        ),
    )(
        big[0],
        big[1],
        big[2],
        delta_index,
        big2[0],
        big2[1],
        big2[2],
        big2[3],
        well_diag.reshape(1, nwells),
        perf_well.reshape(1, 1, nperf),
        perf_cell.reshape(1, 1, nperf),
        perf_coef.reshape(steps, 2, comps, nperf),
    )
    result = result.reshape(steps, comps, nch, nx, LANES)
    return jnp.swapaxes(result, -3, -2).reshape(steps, comps, nx, ny)


def solution(mesh):
    ngx, ngy = mesh.shape["gx"], mesh.shape["gy"]
    return jax.shard_map(
        functools.partial(local, ngx, ngy),
        mesh=mesh,
        in_specs=(
            P(None, "gx", "gy"),
            P(None, "gx", "gy"),
            P(None, None, "gx", "gy"),
            P(),
            P(None, None, None, "gx", "gy"),
            P(None, None, "gx", "gy"),
            P(None, None, None, "gx", "gy"),
            P(None, "gx", "gy"),
            P("gx"),
            P("gx", "gy", None),
            P("gx", "gy", None),
            P(None, None, None, "gx", "gy", None),
        ),
        out_specs=P(None, None, "gx", "gy"),
        check_vma=False,
    )
```

```python
import functools

import jax
import jax.numpy as jnp
from jax import lax
from jax.experimental import pallas as pl
from jax.experimental.pallas import tpu as pltpu
from jax.sharding import PartitionSpec as P

BATCH = 3
LANES = 128
MESH = pl.DeviceIdType.MESH


def split3(x):
    a = x.astype(jnp.bfloat16)
    rest = x - a.astype(jnp.float32)
    b = rest.astype(jnp.bfloat16)
    c = (rest - b.astype(jnp.float32)).astype(jnp.bfloat16)
    return jnp.concatenate([a, b, c], axis=0)


def exact_dot(x, sel, transposed=False):
    rows = x.shape[0]
    dims = (((1,), (1 if transposed else 0,)), ((), ()))
    out = lax.dot_general(split3(x), sel, dims, preferred_element_type=jnp.float32)
    return out[:rows] + out[rows : 2 * rows] + out[2 * rows :]


def kernel(
    ngx,
    ngy,
    comps,
    nx,
    nch,
    nwells,
    steps,
    base_hbm,
    weight_hbm,
    deltas_hbm,
    index_hbm,
    diag_hbm,
    precond_hbm,
    face_hbm,
    accum_hbm,
    wdiag_hbm,
    pwell_hbm,
    pcell_hbm,
    pcoef_hbm,
    out_ref,
    base,
    weight,
    deltas,
    diag,
    precond,
    face,
    accum,
    index_ref,
    wdiag_ref,
    pwell_ref,
    pcell_ref,
    pcoef_ref,
    acc,
    edge,
    xlo_out,
    xhi_out,
    ylo_out,
    yhi_out,
    xlo_in,
    xhi_in,
    ylo_in,
    yhi_in,
    gy_buf,
    gx_buf,
    load_sem,
    send_sem,
    xlo_sem,
    xhi_sem,
    ylo_sem,
    yhi_sem,
    gy_sem,
    gx_sem,
):
    rows = nx * nch
    cells = (comps, rows, LANES)
    flat = (comps * rows, LANES)
    mx = lax.axis_index("gx")
    my = lax.axis_index("gy")
    has_xlo, has_xhi = mx > 0, mx < ngx - 1
    has_ylo, has_yhi = my > 0, my < ngy - 1

    barrier = pltpu.get_barrier_semaphore()
    for d in range(1, ngx):
        pl.semaphore_signal(
            barrier, inc=1, device_id=(lax.rem(mx + d, ngx), my), device_id_type=MESH
        )
    for d in range(1, ngy):
        pl.semaphore_signal(
            barrier, inc=1, device_id=(mx, lax.rem(my + d, ngy)), device_id_type=MESH
        )

    loads = []
    order = (
        (pcell_hbm, pcell_ref),
        (pwell_hbm, pwell_ref),
        (index_hbm, index_ref),
        (wdiag_hbm, wdiag_ref),
        (pcoef_hbm, pcoef_ref),
        (base_hbm, base),
        (weight_hbm, weight),
        (deltas_hbm, deltas),
        (precond_hbm, precond),
        (face_hbm, face),
        (diag_hbm, diag),
        (accum_hbm, accum),
    )
    for n, (src, dst) in enumerate(order):
        cp = pltpu.make_async_copy(src, dst, load_sem.at[n])
        cp.start()
        loads.append(cp)

    @pl.when(jnp.logical_not(has_xlo))
    def _():
        xlo_in[...] = jnp.zeros_like(xlo_in)

    @pl.when(jnp.logical_not(has_xhi))
    def _():
        xhi_in[...] = jnp.zeros_like(xhi_in)

    @pl.when(jnp.logical_not(has_ylo))
    def _():
        ylo_in[...] = jnp.zeros_like(ylo_in)

    @pl.when(jnp.logical_not(has_yhi))
    def _():
        yhi_in[...] = jnp.zeros_like(yhi_in)

    loads[0].wait()
    loads[1].wait()
    pcell = pcell_ref[0]
    length_y = nch * LANES
    p_lane = lax.rem(pcell, LANES)
    p_row = lax.rem(lax.div(pcell, LANES), nch) * nx + lax.div(pcell, length_y)
    nperf = pcell.shape[-1]
    lane_sel = (
        (lax.broadcasted_iota(jnp.int32, (LANES, nperf), 0) == p_lane)
        .astype(jnp.float32)
        .astype(jnp.bfloat16)
    )
    row_mask = lax.broadcasted_iota(jnp.int32, (rows, nperf), 0) == p_row
    well_mask = lax.broadcasted_iota(jnp.int32, (LANES, nperf), 0) == pwell_ref[0]
    well_sel = well_mask.astype(jnp.float32).astype(jnp.bfloat16)
    lane_ids = lax.broadcasted_iota(jnp.int32, (1, rows, LANES), 2)
    row_ids = lax.broadcasted_iota(jnp.int32, (1, rows, LANES), 1)
    sub_ids = lax.broadcasted_iota(jnp.int32, (8, LANES), 0)
    x_ids = lax.rem(row_ids, nx)

    for n in (2, 3, 4, 5, 6, 7):
        loads[n].wait()
    states = []
    running = base[...]
    for k in range(steps):
        picked = [
            deltas[index_ref[k, c], c].astype(jnp.float32)[None] for c in range(comps)
        ]
        running = running + jnp.concatenate(picked, axis=0)
        states.append(running)

    def spread(c_row):
        full = jnp.where(row_mask[None], c_row[:, None, :], jnp.float32(0.0))
        return full.reshape(comps * rows, nperf)

    def apply_precond(v):
        total = precond[:, 0] * v[0][None]
        for j in range(1, comps):
            total = total + precond[:, j] * v[j][None]
        return total

    def neighbour_copy(src, dst, sem_out, sem_in, target):
        return pltpu.make_async_remote_copy(
            src_ref=src,
            dst_ref=dst,
            send_sem=sem_out,
            recv_sem=sem_in,
            device_id=target,
            device_id_type=MESH,
        )

    def wait_bytes(ref, sem):
        pltpu.make_async_copy(ref, ref, sem).wait()

    def operator(k, rnd, slots, vs, row_w, col_w, grams, gx_rnd):
        picked = exact_dot(jnp.concatenate([v.reshape(flat) for v in vs], axis=0), lane_sel)
        weighted = jnp.zeros((8, nperf), jnp.float32)
        for n in range(len(vs)):
            part = picked[n * comps * rows : (n + 1) * comps * rows]
            part = jnp.sum(row_w * part, axis=0, keepdims=True)
            weighted = jnp.where(sub_ids == n, part, weighted)
        message = add_grams(exact_dot(weighted, well_sel, transposed=True), grams)
        if rnd == 0:
            pl.semaphore_wait(barrier, ngx + ngy - 2)
        start_gy(rnd, message)
        kept = []
        for slot, v in zip(slots, vs):
            kept.append(send_halos(k, slot, v))

        for n, v in enumerate(vs):
            f_hi, f_lo, from_y = kept[n]
            total = diag[k, 0] * v[0][None]
            for j in range(1, comps):
                total = total + diag[k, j] * v[j][None]
            down = jnp.concatenate([f_hi[:, rows - 1 :], f_hi[:, : rows - 1]], axis=1)
            up = jnp.concatenate([f_lo[:, 1:], f_lo[:, :1]], axis=1)
            total = total - from_y
            total = total - jnp.where(x_ids == 0, 0.0, down)
            total = total - jnp.where(x_ids == nx - 1, 0.0, up)
            acc[n] = total.reshape(flat)

        for slot in slots:

            @pl.when(has_xlo)
            def _(slot=slot):
                wait_bytes(xlo_in.at[slot], xlo_sem.at[slot])

            @pl.when(has_xhi)
            def _(slot=slot):
                wait_bytes(xhi_in.at[slot], xhi_sem.at[slot])

            @pl.when(has_ylo)
            def _(slot=slot):
                wait_bytes(ylo_in.at[slot], ylo_sem.at[slot])

            @pl.when(has_yhi)
            def _(slot=slot):
                wait_bytes(yhi_in.at[slot], yhi_sem.at[slot])

        for n, slot in enumerate(slots):
            mine = acc.at[n]
            lo_rows = pl.ds(0, comps * nch, stride=nx)
            hi_rows = pl.ds(nx - 1, comps * nch, stride=nx)
            mine[lo_rows, :] = mine[lo_rows, :] - xlo_in[slot]
            mine[hi_rows, :] = mine[hi_rows, :] - xhi_in[slot]
            for c in range(comps):
                first = pl.ds(c * rows, nx)
                last = pl.ds(c * rows + rows - nx, nx)
                part = pl.ds(c * nx, nx)
                mine[first, :] = mine[first, :] - ylo_in[slot, part, :]
                mine[last, :] = mine[last, :] - yhi_in[slot, part, :]

        summed = end_gy(rnd)
        if grams is not None:
            start_gx(gx_rnd, summed)
        per_perf = exact_dot(summed * inv_well, well_sel)
        moved = [col_w * per_perf[n : n + 1] for n in range(len(vs))]
        moved = exact_dot(jnp.concatenate(moved, axis=0), lane_sel, transposed=True)
        size = comps * rows
        return [
            (acc[n] - moved[n * size : (n + 1) * size]).reshape(cells) for n in range(len(vs))
        ]

    def send_halos(k, slot, v):
        f_hi = face[k, 1] * v
        edge[0] = f_hi.reshape(flat)
        xhi_out[slot] = edge[0, pl.ds(nx - 1, comps * nch, stride=nx), :]

        @pl.when(has_xhi)
        def _():
            neighbour_copy(
                xhi_out.at[slot], xlo_in.at[slot], send_sem.at[0], xlo_sem.at[slot], (mx + 1, my)
            ).start()

        f_lo = face[k, 0] * v
        edge[1] = f_lo.reshape(flat)
        xlo_out[slot] = edge[1, pl.ds(0, comps * nch, stride=nx), :]

        @pl.when(has_xlo)
        def _():
            neighbour_copy(
                xlo_out.at[slot], xhi_in.at[slot], send_sem.at[1], xhi_sem.at[slot], (mx - 1, my)
            ).start()

        g = pltpu.roll((face[k, 3] * v).reshape(flat), 1, axis=1).reshape(cells)
        wrap = jnp.concatenate([g[:, rows - nx :], g[:, : rows - nx]], axis=1)
        is_lane = lane_ids == 0
        is_rim = jnp.logical_and(is_lane, row_ids < nx)
        yhi_out[slot] = jnp.where(is_lane[:, :nx], wrap[:, :nx], 0.0).reshape(comps * nx, LANES)

        @pl.when(has_yhi)
        def _():
            neighbour_copy(
                yhi_out.at[slot], ylo_in.at[slot], send_sem.at[2], ylo_sem.at[slot], (mx, my + 1)
            ).start()

        from_ylo = jnp.where(is_rim, 0.0, jnp.where(is_lane, wrap, g))
        g = pltpu.roll((face[k, 2] * v).reshape(flat), LANES - 1, axis=1).reshape(cells)
        wrap = jnp.concatenate([g[:, nx:], g[:, :nx]], axis=1)
        is_lane = lane_ids == LANES - 1
        is_rim = jnp.logical_and(is_lane, row_ids >= rows - nx)
        ylo_out[slot] = jnp.where(is_lane[:, rows - nx :], wrap[:, rows - nx :], 0.0).reshape(
            comps * nx, LANES
        )

        @pl.when(has_ylo)
        def _():
            neighbour_copy(
                ylo_out.at[slot], yhi_in.at[slot], send_sem.at[3], yhi_sem.at[slot], (mx, my - 1)
            ).start()

        return f_hi, f_lo, from_ylo + jnp.where(is_rim, 0.0, jnp.where(is_lane, wrap, g))

    def grams_of(q0, q1, q2):
        return (q0 * q1, q1 * q1, q0 * q2, q1 * q2, q2 * q2)

    def add_grams(message, grams):
        if grams is None:
            return message
        for n, g in enumerate(grams):
            total = jnp.sum(g.reshape(flat), axis=0, keepdims=True)
            message = jnp.where(sub_ids == BATCH + n, total, message)
        return message

    def start_gy(rnd, message):
        gy_buf[rnd, my] = message
        for d in range(1, ngy):
            neighbour_copy(
                gy_buf.at[rnd, my],
                gy_buf.at[rnd, my],
                send_sem.at[4],
                gy_sem.at[rnd],
                (mx, lax.rem(my + d, ngy)),
            ).start()

    def end_gy(rnd):
        wait_bytes(gy_buf.at[rnd, pl.ds(0, ngy - 1)], gy_sem.at[rnd])
        return jnp.sum(gy_buf[rnd], axis=0)

    def start_gx(rnd, message):
        gx_buf[rnd, mx] = message
        for d in range(1, ngx):
            neighbour_copy(
                gx_buf.at[rnd, mx],
                gx_buf.at[rnd, mx],
                send_sem.at[5],
                gx_sem.at[rnd],
                (lax.rem(mx + d, ngx), my),
            ).start()

    def end_gx(rnd):
        wait_bytes(gx_buf.at[rnd, pl.ds(0, ngx - 1)], gx_sem.at[rnd])
        totals = jnp.sum(jnp.sum(gx_buf[rnd], axis=0), axis=1, keepdims=True)
        g01, g11, g02, g12, g22 = (totals[BATCH + n : BATCH + n + 1] for n in range(5))
        first = g01 / g11
        second = (
            first * (first * g12 - g02) / (g11 - 2.0 * first * g12 + first * first * g22)
        )
        return (first + second)[None], (first * second)[None]

    inv_well = jnp.concatenate(
        [jnp.float32(1.0) / wdiag_ref[...], jnp.ones((1, LANES - nwells), jnp.float32)], axis=1
    )

    for n in (8, 9, 10, 11):
        loads[n].wait()

    gy_rnd = gx_rnd = slot = 0
    late = None
    for k in range(steps - 1, -1, -1):
        row_w = spread(pcoef_ref[k, 0])
        col_w = spread(pcoef_ref[k, 1])
        v0 = weight[...] * states[k]
        if late is None:
            u0 = apply_precond(v0)
            (v1,) = operator(k, gy_rnd, [slot], [u0], row_w, col_w, None, None)
            slot += 1
            u1 = apply_precond(v1)
            (v2,) = operator(k, gy_rnd + 1, [slot], [u1], row_w, col_w, None, None)
        else:
            grams, part, p0, p1 = late
            starts = [v0 + accum[...] * part, accum[...] * p0, accum[...] * p1]
            firsts = [apply_precond(v) for v in starts]
            slots = [slot + n for n in range(BATCH)]
            images = operator(k, gy_rnd, slots, firsts, row_w, col_w, grams, gx_rnd)
            seconds = [apply_precond(v) for v in images]
            slots = [slot + BATCH + n for n in range(BATCH)]
            later = operator(k, gy_rnd + 1, slots, seconds, row_w, col_w, None, None)
            slot += 2 * BATCH - 1
            both, prod = end_gx(gx_rnd)
            gx_rnd += 1
            out_ref[k + 1] = part + both * p0 - prod * p1
            v0, u0, v1, u1, v2 = (
                a + both * b - prod * c
                for a, b, c in (starts, firsts, images, seconds, later)
            )
        gy_rnd += 1
        u2 = apply_precond(v2)
        grams = grams_of(v0, v1, v2)
        (v3,) = operator(k, gy_rnd + 1, [slot + 1], [u2], row_w, col_w, grams, gx_rnd)
        u3 = apply_precond(v3)
        (v4,) = operator(k, gy_rnd + 2, [slot + 2], [u3], row_w, col_w, None, None)
        gy_rnd += 3
        slot += 3
        both, prod = end_gx(gx_rnd)
        gx_rnd += 1
        q0 = v0 - both * v1 + prod * v2
        q1 = v1 - both * v2 + prod * v3
        q2 = v2 - both * v3 + prod * v4
        part = both * u0 - prod * u1
        p0 = u0 - both * u1 + prod * u2
        p1 = u1 - both * u2 + prod * u3
        late = grams_of(q0, q1, q2), part, p0, p1
    grams, part, p0, p1 = late
    start_gy(gy_rnd, add_grams(jnp.zeros((8, LANES), jnp.float32), grams))
    start_gx(gx_rnd, end_gy(gy_rnd))
    both, prod = end_gx(gx_rnd)
    out_ref[0] = part + both * p0 - prod * p1

    @pl.when(has_xhi)
    def _():
        wait_bytes(xhi_out, send_sem.at[0])

    @pl.when(has_xlo)
    def _():
        wait_bytes(xlo_out, send_sem.at[1])

    @pl.when(has_yhi)
    def _():
        wait_bytes(yhi_out, send_sem.at[2])

    @pl.when(has_ylo)
    def _():
        wait_bytes(ylo_out, send_sem.at[3])

    wait_bytes(gy_buf.at[:, pl.ds(0, ngy - 1)], send_sem.at[4])
    wait_bytes(gx_buf.at[:, pl.ds(0, ngx - 1)], send_sem.at[5])


def to_rows(x):
    lead = x.shape[:-2]
    nx, ny = x.shape[-2:]
    x = x.reshape(*lead, nx, ny // LANES, LANES)
    return jnp.swapaxes(x, -3, -2).reshape(*lead, nx * (ny // LANES), LANES)


def local(
    ngx,
    ngy,
    base_state,
    misfit_weight,
    state_deltas,
    delta_index,
    diag_block,
    precond,
    face_coupling,
    accumulation,
    well_diag,
    perf_well,
    perf_cell,
    perf_coef,
):
    comps, nx, ny = base_state.shape
    nch = ny // LANES
    rows = nx * nch
    steps = diag_block.shape[0]
    nwells = well_diag.shape[0]
    nperf = perf_cell.shape[-1]
    slots = 4 + (steps - 1) * (2 * BATCH + 2)
    gy_rounds = 4 * steps + 1
    gx_rounds = 2 * steps
    f32 = jnp.float32
    big = [to_rows(a) for a in (base_state, misfit_weight, state_deltas)]
    big2 = [to_rows(a) for a in (diag_block, precond, face_coupling, accumulation)]
    any_spec = pl.BlockSpec(memory_space=pl.ANY)
    vmem = pl.BlockSpec(memory_space=pltpu.VMEM)
    xh = pltpu.VMEM((slots, comps * nch, LANES), f32)
    yh = pltpu.VMEM((slots, comps * nx, LANES), f32)
    result = pl.pallas_call(
        functools.partial(kernel, ngx, ngy, comps, nx, nch, nwells, steps),
        out_shape=jax.ShapeDtypeStruct((steps, comps, rows, LANES), f32),
        in_specs=[any_spec] * 12,
        out_specs=vmem,
        scratch_shapes=[
            pltpu.VMEM(big[0].shape, f32),
            pltpu.VMEM(big[1].shape, f32),
            pltpu.VMEM(big[2].shape, big[2].dtype),
            pltpu.VMEM(big2[0].shape, f32),
            pltpu.VMEM(big2[1].shape, f32),
            pltpu.VMEM(big2[2].shape, f32),
            pltpu.VMEM(big2[3].shape, f32),
            pltpu.SMEM(delta_index.shape, jnp.int32),
            pltpu.VMEM((1, nwells), f32),
            pltpu.VMEM((1, 1, nperf), jnp.int32),
            pltpu.VMEM((1, 1, nperf), jnp.int32),
            pltpu.VMEM((steps, 2, comps, nperf), f32),
            pltpu.VMEM((BATCH, comps * rows, LANES), f32),
            pltpu.VMEM((2, comps * rows, LANES), f32),
            xh,
            xh,
            yh,
            yh,
            xh,
            xh,
            yh,
            yh,
            pltpu.VMEM((gy_rounds, ngy, 8, LANES), f32),
            pltpu.VMEM((gx_rounds, ngx, 8, LANES), f32),
            pltpu.SemaphoreType.DMA((12,)),
            pltpu.SemaphoreType.DMA((6,)),
            pltpu.SemaphoreType.DMA((slots,)),
            pltpu.SemaphoreType.DMA((slots,)),
            pltpu.SemaphoreType.DMA((slots,)),
            pltpu.SemaphoreType.DMA((slots,)),
            pltpu.SemaphoreType.DMA((gy_rounds,)),
            pltpu.SemaphoreType.DMA((gx_rounds,)),
        ],
        compiler_params=pltpu.CompilerParams(
            collective_id=0, has_side_effects=True, vmem_limit_bytes=60 * 1024 * 1024
        ),
    )(
        big[0],
        big[1],
        big[2],
        delta_index,
        big2[0],
        big2[1],
        big2[2],
        big2[3],
        well_diag.reshape(1, nwells),
        perf_well.reshape(1, 1, nperf),
        perf_cell.reshape(1, 1, nperf),
        perf_coef.reshape(steps, 2, comps, nperf),
    )
    result = result.reshape(steps, comps, nch, nx, LANES)
    return jnp.swapaxes(result, -3, -2).reshape(steps, comps, nx, ny)


def solution(mesh):
    ngx, ngy = mesh.shape["gx"], mesh.shape["gy"]
    return jax.shard_map(
        functools.partial(local, ngx, ngy),
        mesh=mesh,
        in_specs=(
            P(None, "gx", "gy"),
            P(None, "gx", "gy"),
            P(None, None, "gx", "gy"),
            P(),
            P(None, None, None, "gx", "gy"),
            P(None, None, "gx", "gy"),
            P(None, None, None, "gx", "gy"),
            P(None, "gx", "gy"),
            P("gx"),
            P("gx", "gy", None),
            P("gx", "gy", None),
            P(None, None, None, "gx", "gy", None),
        ),
        out_specs=P(None, None, "gx", "gy"),
        check_vma=False,
    )
```
